32 devices in a mesh: dp: 2 (over y), latent: 16 (over z, x, core).
Axes of the slice: x: 2, y: 2, z: 4, core: 2. Of those that a mesh axis runs over, the one named last changes fastest.
Arguments:
- resid: bfloat16 [128, 4608], P('dp'), may hold values from -24 to 24
- enc_weight: bfloat16 [4608, 131072], P(None, ('dp', 'latent')), may hold values from -0.09375 to 0.09375
- enc_bias: float32 [131072], P(('dp', 'latent')), may hold values from -3 to 3
- thresholds: float32 [131072], P(('dp', 'latent')), may hold values from 0.5 to 3
- dec_weight: bfloat16 [131072, 4608], P(('dp', 'latent')), may hold values from -0.09375 to 0.09375
- dec_bias: float32 [4608], replicated, may hold values from -7 to 7
- refusal_ids: int32 [16], replicated, may hold values from 0 to 131071, as said below
- clamp_levels: int32 [16], replicated, may hold values from 1 to 8
Outputs:
- steered: bfloat16 [128, 4608], P('dp')
The draws below stay inside these ranges and needn't reach their ends.
Inputs may be any that keep to these rules, and one draw needn't show every extreme that they name: `refusal_ids`: an index may be named more than once, with different clamp levels.
All inputs are finite; a program needn't handle non-finite values.
Results may differ from the reference program's by a relative error of at most 0.0052.
Values may be sent and summed in bfloat16 or wider, within the bound.
A program may use at most 128 MiB of HBM per device.

```python
import math
import jax
import jax.numpy as jnp
from jax import lax

D = 4608
LATENTS = 131072
K = 16
TOKENS = 128


def scales_of(key, length, low, high, wobble):
    log_ramp = jnp.linspace(math.log(low), math.log(high), length)
    return jnp.exp(log_ramp + jax.random.uniform(key, (length,), jnp.float32, -wobble, wobble))


def draw_resid(key, part):
    k_base, k_rows, k_cols = jax.random.split(key, 3)
    values = jnp.clip(jax.random.normal(k_base, (TOKENS, D), jnp.float32), -4.0, 4.0)
    row_scale = jnp.exp(jax.random.uniform(k_rows, (TOKENS, 1), jnp.float32, math.log(0.3), math.log(3.0)))
    col_scale = scales_of(k_cols, D, 0.4, 1.2, 0.5)
    return (values * row_scale * col_scale[None, :]).astype(jnp.bfloat16)


def draw_dec_bias(key, part):
    k_base, k_cols = jax.random.split(key, 2)
    values = jnp.clip(jax.random.normal(k_base, (D,), jnp.float32), -4.0, 4.0)
    return values * scales_of(k_cols, D, 0.3, 1.0, 0.5)


def refusal_table(key):
    k_ids, k_src, k_first, k_up, k_down, k_rest = jax.random.split(jax.random.fold_in(key, 31), 6)
    half_count = K // 2
    quarter_count = K // 4
    id_values = jax.random.randint(k_ids, (K,), 0, LATENTS, dtype=jnp.int32)
    source_slots = jax.random.permutation(k_src, half_count)[:quarter_count].astype(jnp.int32)
    copy_slots = half_count + jnp.arange(quarter_count, dtype=jnp.int32)
    id_values = id_values.at[copy_slots].set(id_values[source_slots])
    id_values = id_values.at[K - 2].set(0).at[K - 1].set(LATENTS - 1)
    level_values = jax.random.randint(k_rest, (K,), 1, 9, dtype=jnp.int32)
    first_levels = jax.random.randint(k_first, (half_count,), 3, 7, dtype=jnp.int32)
    level_values = level_values.at[:half_count].set(first_levels)
    source_levels = first_levels[source_slots]
    raised = jax.random.randint(k_up, (quarter_count,), source_levels + 2, 9, dtype=jnp.int32)
    lowered = jax.random.randint(k_down, (quarter_count,), 1, source_levels - 1, dtype=jnp.int32)
    raise_mask = jnp.arange(quarter_count, dtype=jnp.int32) % 2 == 0
    level_values = level_values.at[copy_slots].set(jnp.where(raise_mask, raised, lowered))
    level_values = level_values.at[K - 2].set(1).at[K - 1].set(8)
    return (id_values, level_values)


def draw_refusal_ids(key, part):
    return refusal_table(key)[0]


def draw_clamp_levels(key, part):
    return refusal_table(key)[1]


def block_levels(own_key, extent, cuts, low, high):
    factor_of = 1.0
    for position, blocks in cuts:
        draws = jax.random.uniform(jax.random.fold_in(jax.random.fold_in(own_key, 6), position), (blocks,), jnp.float32, low / len(cuts), high / len(cuts))
        factor_of = factor_of * jnp.repeat(jnp.exp(draws), extent[position] // blocks).reshape((-1,) + (1,) * (len(extent) - 1 - position))
    return factor_of


def bell_draw(own_key, dims, spread, most, pieces=(), held_as=jnp.bfloat16):
    array = jax.random.normal(own_key, dims, jnp.float32) * spread
    if len(pieces) > 0:
        array = block_levels(own_key, dims, pieces, -0.22, 0.18) * array
    return jnp.clip(array, min=-most, max=most).astype(held_as)


def setup_inputs(seed: int = 0) -> dict:
    keys = jax.random.split(jax.random.key(seed), 9)
    return {
        "resid": draw_resid(jax.random.fold_in(keys[8], 71), 0),
        "enc_weight": bell_draw(keys[1], (D, LATENTS), D ** -0.5, 0.09375, ((1, 32),)),
        "enc_bias": bell_draw(keys[2], (LATENTS,), 0.5, 3.0, ((0, 32),), jnp.float32),
        "thresholds": jnp.clip(jnp.exp(math.log(3.0) - 1.7917595 * jax.random.uniform(keys[3], (LATENTS,), jnp.float32) ** block_levels(keys[3], (LATENTS,), ((0, 32),), -0.2, 0.2)), 0.5, 3.0),
        "dec_weight": bell_draw(keys[4], (LATENTS, D), D ** -0.5, 0.09375, ((0, 32),)),
        "dec_bias": draw_dec_bias(jax.random.fold_in(keys[8], 71), 0),
        "refusal_ids": draw_refusal_ids(jax.random.fold_in(keys[8], 71), 0),
        "clamp_levels": draw_clamp_levels(jax.random.fold_in(keys[8], 71), 0),
    }


gate_width = 0.1
norm_eps = 1e-06

def gate_latents(pre_acts, thresh_part):
    return pre_acts * jax.nn.sigmoid((pre_acts - thresh_part) / gate_width)

def clamp_block(activations, columns, refusal_ids, clamp_levels, thresh_part):
    matched = refusal_ids[:, None] == columns[None, :]
    targets_all = clamp_levels.astype(jnp.float32)[:, None] * thresh_part[None, :]
    targets = lax.optimization_barrier(jnp.max(jnp.where(matched, targets_all, -1.0), axis=0))
    is_named = jnp.any(matched, axis=0)
    return jnp.where(is_named[None, :], jnp.maximum(activations, targets[None, :]), activations)

def reference(resid, enc_weight, enc_bias, thresholds, dec_weight, dec_bias, refusal_ids, clamp_levels):
    block_count = 16
    block_width = LATENTS // block_count

    def one_block(running, block_index):
        offset = block_index * block_width
        w_enc = lax.dynamic_slice_in_dim(enc_weight, offset, block_width, 1)
        w_dec = lax.dynamic_slice_in_dim(dec_weight, offset, block_width, 0)
        bias_part = lax.dynamic_slice_in_dim(enc_bias, offset, block_width, 0)
        thresh_part = lax.dynamic_slice_in_dim(thresholds, offset, block_width, 0)
        pre_acts = jnp.dot(resid, w_enc, preferred_element_type=jnp.float32) + bias_part
        columns = offset + jnp.arange(block_width, dtype=jnp.int32)
        clamped = clamp_block(gate_latents(pre_acts, thresh_part), columns, refusal_ids, clamp_levels, thresh_part).astype(jnp.bfloat16)
        return (running + jnp.dot(clamped, w_dec, preferred_element_type=jnp.float32), None)
    recon, _ = lax.scan(one_block, jnp.zeros((TOKENS, D), jnp.float32), jnp.arange(block_count, dtype=jnp.int32))
    recon = recon + dec_bias
    in_sq = lax.optimization_barrier(jnp.sum(jnp.square(resid.astype(jnp.float32)), axis=1, keepdims=True))
    out_sq = lax.optimization_barrier(jnp.sum(jnp.square(recon), axis=1, keepdims=True))
    return (recon * jnp.sqrt((in_sq + norm_eps) / (out_sq + norm_eps))).astype(jnp.bfloat16)
```

```python
import functools

import jax
import jax.numpy as jnp
from jax import lax
from jax.experimental import pallas as pl
from jax.experimental.pallas import tpu as pltpu
from jax.sharding import PartitionSpec as P

gate_width = 0.1
norm_eps = 1e-06
no_target = -3.0e38

MESH = pl.DeviceIdType.MESH
WIDTH = 512
HALF = 256
QUART = 128
PIECES = 3
LAGS = (1, 2, 3, 4, 5)


def kernel(
    sizes,
    ids_ref,
    levels_ref,
    resid_ref,
    enc_ref,
    bias_ref,
    thresh_ref,
    dec_ref,
    dbias_ref,
    out_ref,
    wbuf,
    xfull,
    acts,
    targ,
    own,
    pair_tx,
    pair_rx,
    y_own,
    y_tx,
    y_rx,
    x_own,
    x_tx,
    x_rx,
    z_tx,
    z_rx,
    recon,
    w_sem,
    loc_sem,
    g_ssem,
    g_rsem,
    f_ssem,
    f_rsem,
    pair_ssem,
    pair_rsem,
    y_ssem,
    y_rsem,
    x_ssem,
    x_rsem,
    z_ssem,
    z_rsem,
    a_ssem,
    a_rsem,
    b_ssem,
    b_rsem,
):
    n_dp, n_z, n_x, slots = sizes
    rows, width = resid_ref.shape
    lat_dev = enc_ref.shape[1]
    n_enc = lat_dev // WIDTH
    n_dec = width // WIDTH
    z_rows = rows // n_z
    h_rows = rows // 2
    piece = width // PIECES
    dp = lax.axis_index("dp")
    lat = lax.axis_index("latent")
    core = lax.rem(lat, 2)
    chip = lax.div(lat, 2)
    x = lax.rem(chip, n_x)
    z = lax.div(chip, n_x)
    xh = lax.rem(x, 2)
    x_pair = x + 1 - 2 * xh

    def lat_of(z_, x_, core_):
        return (z_ * n_x + x_) * 2 + core_

    partner = (dp, lat_of(z, x, 1 - core))
    dp_peers = [(lax.rem(dp + o, n_dp), lat) for o in range(1, n_dp)]
    x_index = [lax.rem(x + o, n_x) for o in range(1, n_x)]
    x_peers = [(dp, lat_of(z, xo, core)) for xo in x_index]
    z_index = [lax.rem(z + o, n_z) for o in range(1, n_z)]
    z_peers = [(dp, lat_of(zo, x, core)) for zo in z_index]
    fwd_peers = [
        partner,
        (dp, lat_of(z, x_pair, core)),
        (dp, lat_of(z, x_pair, 1 - core)),
    ]

    def enc_copy(i):
        cols = pl.ds(pl.multiple_of(i * WIDTH, WIDTH), WIDTH)
        return pltpu.make_async_copy(enc_ref.at[:, cols], wbuf.at[i], w_sem.at[i])

    def dec_slot(j):
        return lax.rem(j + slots - (slots - n_enc), slots) if slots > n_enc else lax.rem(j, slots)

    def dec_copy(j):
        cols = pl.ds(pl.multiple_of(j * WIDTH, WIDTH), WIDTH)
        s = dec_slot(j)
        return pltpu.make_async_copy(
            dec_ref.at[:, cols], wbuf.at[s, pl.ds(0, lat_dev)], w_sem.at[s]
        )

    def remote(src, dst, ssem, rsem, device):
        return pltpu.make_async_remote_copy(
            src_ref=src, dst_ref=dst, send_sem=ssem, recv_sem=rsem,
            device_id=device, device_id_type=MESH,
        )

    def start_enc(i, _):
        enc_copy(i).start()
        return 0

    lax.fori_loop(0, n_enc, start_enc, 0)
    ahead = slots - n_enc
    for j in range(ahead):
        dec_copy(j).start()
    own_rows = pl.ds(pl.multiple_of(dp * rows, rows), rows)
    local = pltpu.make_async_copy(resid_ref, xfull.at[own_rows], loc_sem)
    local.start()

    barrier = pltpu.get_barrier_semaphore()
    greeted = dp_peers + x_peers + z_peers + [fwd_peers[0], fwd_peers[2]]
    for device in greeted:
        pl.semaphore_signal(barrier, inc=1, device_id=device, device_id_type=MESH)
    pl.semaphore_wait(barrier, len(greeted))

    def gather(o, s):
        cols = pl.ds(s * piece, piece)
        src_rows = pl.ds(pl.multiple_of(core * h_rows, 16), h_rows)
        dst_rows = pl.ds(pl.multiple_of(dp * rows + core * h_rows, 16), h_rows)
        return remote(
            resid_ref.at[src_rows, cols], xfull.at[dst_rows, cols],
            g_ssem.at[o, s], g_rsem.at[o, s], dp_peers[o],
        )

    def forward(o, s):
        cols = pl.ds(s * piece, piece)
        origin = lax.rem(dp + n_dp - (o + 1), n_dp)
        r = pl.ds(pl.multiple_of(origin * rows + core * h_rows, 16), h_rows)
        return remote(
            xfull.at[r, cols], xfull.at[r, cols], f_ssem.at[o, s], f_rsem.at[o, s], partner
        )

    pairs = [(o, s) for s in range(PIECES) for o in range(n_dp - 1)]
    for o, s in pairs:
        gather(o, s).start()

    first_col = (dp * lax.axis_size("latent") + lat) * lat_dev
    columns = first_col + lax.broadcasted_iota(jnp.int32, (1, lat_dev), 1)
    thresh_all = thresh_ref[...]
    targets = jnp.full((1, lat_dev), no_target, jnp.float32)
    for k in range(ids_ref.shape[0]):
        level = levels_ref[k].astype(jnp.float32)
        targets = jnp.where(
            columns == ids_ref[k], jnp.maximum(targets, level * thresh_all), targets
        )
    targ[...] = targets

    for o, s in pairs:
        gather(o, s).wait_recv()
        forward(o, s).start()
    local.wait()
    for o, s in pairs:
        forward(o, s).wait_recv()

    def encode(i, _):
        cols = pl.ds(pl.multiple_of(i * WIDTH, WIDTH), WIDTH)
        enc_copy(i).wait()
        pre = jnp.dot(xfull[...], wbuf[i], preferred_element_type=jnp.float32) + bias_ref[:, cols]
        act = pre * jax.nn.sigmoid((pre - thresh_ref[:, cols]) / gate_width)
        acts[:, cols] = jnp.maximum(act, targ[:, cols]).astype(jnp.bfloat16)

        @pl.when(i + ahead < n_dec)
        def _():
            dec_copy(i + ahead).start()

        return 0

    lax.fori_loop(0, n_enc, encode, 0)

    def pair_copy(k):
        return remote(pair_tx.at[k], pair_rx.at[k], pair_ssem.at[k], pair_rsem.at[k], partner)

    def y_copy(k, o):
        return remote(
            y_tx.at[k, o], y_rx.at[k, o], y_ssem.at[k, o], y_rsem.at[k, o], dp_peers[o]
        )

    def x_copy(k, o):
        return remote(x_tx.at[k, o], x_rx.at[k, o], x_ssem.at[k, o], x_rsem.at[k, o], x_peers[o])

    def z_copy(k, o):
        return remote(z_tx.at[k, o], z_rx.at[k, o], z_ssem.at[k, o], z_rsem.at[k, o], z_peers[o])

    def own_cols(k):
        return pl.ds(pl.multiple_of(k * WIDTH + core * HALF + xh * QUART, QUART), QUART)

    def a_copy(k, o):
        ref = recon.at[pl.ds(pl.multiple_of(z * z_rows, 16), z_rows), own_cols(k)]
        return remote(ref, ref, a_ssem.at[k, o], a_rsem.at[k, o], z_peers[o])

    def b_copy(k, o):
        ref = recon.at[:, own_cols(k)]
        return remote(ref, ref, b_ssem.at[k, o], b_rsem.at[k, o], fwd_peers[o])

    def decode(k):
        dec_copy(k).wait()
        part = jnp.dot(
            acts[...], wbuf[dec_slot(k), :lat_dev], preferred_element_type=jnp.float32
        )
        low, high = part[:, :HALF], part[:, HALF:]
        own[lax.rem(k, 2)] = jnp.where(core == 0, low, high)
        pair_tx[k] = jnp.where(core == 0, high, low).astype(jnp.bfloat16)
        pair_copy(k).start()

        if n_enc + ahead < n_dec:

            @pl.when(k + n_enc + ahead < n_dec)
            def _():
                dec_copy(k + n_enc + ahead).start()

    def after_pair(k):
        pair_copy(k).wait_recv()
        slot = lax.rem(k, 2)

        def rows_of(q):
            r = pl.ds(pl.multiple_of(q * rows, rows), rows)
            return own[slot, r] + pair_rx[k, r].astype(jnp.float32)

        for o in range(n_dp - 1):
            y_tx[k, o] = rows_of(dp_peers[o][0]).astype(jnp.bfloat16)
            y_copy(k, o).start()
        y_own[k] = rows_of(dp)

    def after_y(k):
        total = y_own[k]
        for o in range(n_dp - 1):
            y_copy(k, o).wait_recv()
            total = total + y_rx[k, o].astype(jnp.float32)
        halves = (total[:, :QUART], total[:, QUART:])
        for o in range(n_x - 1):
            there = jnp.where(lax.rem(x_index[o], 2) == 0, halves[0], halves[1])
            x_tx[k, o] = there.astype(jnp.bfloat16)
            x_copy(k, o).start()
        x_own[k] = jnp.where(xh == 0, halves[0], halves[1])

    def after_x(k):
        total = x_own[k]
        for o in range(n_x - 1):
            x_copy(k, o).wait_recv()
            total = total + x_rx[k, o].astype(jnp.float32)
        x_own[k] = total
        for o in range(n_z - 1):
            r = pl.ds(pl.multiple_of(z_index[o] * z_rows, z_rows), z_rows)
            z_tx[k, o] = x_own[k, r].astype(jnp.bfloat16)
            z_copy(k, o).start()

    def after_z(k):
        total = x_own[k, pl.ds(pl.multiple_of(z * z_rows, z_rows), z_rows)]
        for o in range(n_z - 1):
            z_copy(k, o).wait_recv()
            total = total + z_rx[k, o].astype(jnp.float32)
        total = total + dbias_ref[:, own_cols(k)]
        r = pl.ds(pl.multiple_of(z * z_rows, 16), z_rows)
        recon[r, own_cols(k)] = total.astype(jnp.bfloat16)
        for o in range(n_z - 1):
            a_copy(k, o).start()

    def after_gather(k):
        for o in range(n_z - 1):
            a_copy(k, o).wait_recv()
        for o in range(3):
            b_copy(k, o).start()

    stages = (after_pair, after_y, after_x, after_z, after_gather)

    def step(it, _):
        @pl.when(it < n_dec)
        def _():
            decode(it)

        for stage, lag in zip(stages, LAGS):

            @pl.when(jnp.logical_and(it >= lag, it < n_dec + lag))
            def _(stage=stage, lag=lag):
                stage(it - lag)

        return 0

    lax.fori_loop(0, n_dec + LAGS[-1], step, 0)

    resid32 = xfull[own_rows].astype(jnp.float32)
    in_sq = jnp.sum(jnp.square(resid32), axis=1, keepdims=True)

    def finish(k, _):
        for o in range(3):
            b_copy(k, o).wait_recv()
        return 0

    lax.fori_loop(0, n_dec, finish, 0)

    full = recon[...].astype(jnp.float32)
    out_sq = jnp.sum(jnp.square(full), axis=1, keepdims=True)
    scale = jnp.sqrt((in_sq + norm_eps) / (out_sq + norm_eps))
    out_ref[...] = (recon[...].astype(jnp.float32) * scale).astype(jnp.bfloat16)

    for o, s in pairs:
        gather(o, s).wait_send()
        forward(o, s).wait_send()

    def sent(k, _):
        pair_copy(k).wait_send()
        for o in range(n_dp - 1):
            y_copy(k, o).wait_send()
        for o in range(n_x - 1):
            x_copy(k, o).wait_send()
        for o in range(n_z - 1):
            z_copy(k, o).wait_send()
            a_copy(k, o).wait_send()
        for o in range(3):
            b_copy(k, o).wait_send()
        return 0

    lax.fori_loop(0, n_dec, sent, 0)


def body(n_dp, n_lat, resid, enc_weight, enc_bias, thresholds, dec_weight, dec_bias, ids, levels):
    rows, width = resid.shape
    lat_dev = enc_weight.shape[1]
    tokens = rows * n_dp
    n_enc, n_dec = lat_dev // WIDTH, width // WIDTH
    n_z = 4
    n_x = n_lat // (2 * n_z)
    slots = n_enc + 1 if tokens <= 256 else n_enc
    z_rows = rows // n_z
    bf16, f32 = jnp.bfloat16, jnp.float32
    dma = pltpu.SemaphoreType.DMA
    anywhere = pl.BlockSpec(memory_space=pl.ANY)
    vmem = pl.BlockSpec(memory_space=pltpu.VMEM)
    smem = pl.BlockSpec(memory_space=pltpu.SMEM)
    return pl.pallas_call(
        functools.partial(kernel, (n_dp, n_z, n_x, slots)),
        out_shape=jax.ShapeDtypeStruct((rows, width), bf16),
        in_specs=[smem, smem, anywhere, anywhere, vmem, vmem, anywhere, vmem],
        out_specs=vmem,
        scratch_shapes=[
            pltpu.VMEM((slots, width, WIDTH), bf16),
            pltpu.VMEM((tokens, width), bf16),
            pltpu.VMEM((tokens, lat_dev), bf16),
            pltpu.VMEM((1, lat_dev), f32),
            pltpu.VMEM((2, tokens, HALF), f32),
            pltpu.VMEM((n_dec, tokens, HALF), bf16),
            pltpu.VMEM((n_dec, tokens, HALF), bf16),
            pltpu.VMEM((n_dec, rows, HALF), f32),
            pltpu.VMEM((n_dec, n_dp - 1, rows, HALF), bf16),
            pltpu.VMEM((n_dec, n_dp - 1, rows, HALF), bf16),
            pltpu.VMEM((n_dec, rows, QUART), f32),
            pltpu.VMEM((n_dec, n_x - 1, rows, QUART), bf16),
            pltpu.VMEM((n_dec, n_x - 1, rows, QUART), bf16),
            pltpu.VMEM((n_dec, n_z - 1, z_rows, QUART), bf16),
            pltpu.VMEM((n_dec, n_z - 1, z_rows, QUART), bf16),
            pltpu.VMEM((rows, width), bf16),
            dma((slots,)),
            dma,
            dma((n_dp - 1, PIECES)),
            dma((n_dp - 1, PIECES)),
            dma((n_dp - 1, PIECES)),
            dma((n_dp - 1, PIECES)),
            dma((n_dec,)),
            dma((n_dec,)),
            dma((n_dec, n_dp - 1)),
            dma((n_dec, n_dp - 1)),
            dma((n_dec, n_x - 1)),
            dma((n_dec, n_x - 1)),
            dma((n_dec, n_z - 1)),
            dma((n_dec, n_z - 1)),
            dma((n_dec, n_z - 1)),
            dma((n_dec, n_z - 1)),
            dma((n_dec, 3)),
            dma((n_dec, 3)),
        ],
        compiler_params=pltpu.CompilerParams(
            collective_id=0, has_side_effects=True, vmem_limit_bytes=60 * 2**20
        ),
    )(
        ids,
        levels,
        resid,
        enc_weight,
        enc_bias.reshape(1, lat_dev),
        thresholds.reshape(1, lat_dev),
        dec_weight,
        dec_bias.reshape(1, width),
    )


def solution(mesh):
    in_specs = (
        P("dp", None),
        P(None, ("dp", "latent")),
        P(("dp", "latent")),
        P(("dp", "latent")),
        P(("dp", "latent"), None),
        P(),
        P(),
        P(),
    )
    return jax.shard_map(
        functools.partial(body, mesh.shape["dp"], mesh.shape["latent"]),
        mesh=mesh,
        in_specs=in_specs,
        out_specs=P("dp", None),
        check_vma=False,
    )
```

```python
import functools

import jax
import jax.numpy as jnp
from jax import lax
from jax.experimental import pallas as pl
from jax.experimental.pallas import tpu as pltpu
from jax.sharding import PartitionSpec as P

gate_width = 0.1
norm_eps = 1e-06
no_target = -3.0e38

MESH = pl.DeviceIdType.MESH
WIDTH = 512
HALF = 256
QUART = 128
PIECES = 3
LAGS = (1, 4, 7, 10, 13)


def kernel(
    sizes,
    ids_ref,
    levels_ref,
    resid_ref,
    enc_ref,
    bias_ref,
    thresh_ref,
    dec_ref,
    dbias_ref,
    out_ref,
    wbuf,
    xfull,
    acts,
    targ,
    own,
    pair_tx,
    pair_rx,
    y_own,
    y_tx,
    y_rx,
    x_own,
    x_tx,
    x_rx,
    z_tx,
    z_rx,
    recon,
    w_sem,
    loc_sem,
    g_ssem,
    g_rsem,
    f_ssem,
    f_rsem,
    pair_ssem,
    pair_rsem,
    y_ssem,
    y_rsem,
    x_ssem,
    x_rsem,
    z_ssem,
    z_rsem,
    a_ssem,
    a_rsem,
    b_ssem,
    b_rsem,
):
    n_dp, n_z, n_x, slots = sizes
    rows, width = resid_ref.shape
    lat_dev = enc_ref.shape[1]
    n_enc = lat_dev // WIDTH
    n_dec = width // WIDTH
    z_rows = rows // n_z
    h_rows = rows // 2
    piece = width // PIECES
    dp = lax.axis_index("dp")
    lat = lax.axis_index("latent")
    core = lax.rem(lat, 2)
    chip = lax.div(lat, 2)
    x = lax.rem(chip, n_x)
    z = lax.div(chip, n_x)
    xh = lax.rem(x, 2)
    x_pair = x + 1 - 2 * xh

    def lat_of(z_, x_, core_):
        return (z_ * n_x + x_) * 2 + core_

    partner = (dp, lat_of(z, x, 1 - core))
    dp_peers = [(lax.rem(dp + o, n_dp), lat) for o in range(1, n_dp)]
    x_index = [lax.rem(x + o, n_x) for o in range(1, n_x)]
    x_peers = [(dp, lat_of(z, xo, core)) for xo in x_index]
    z_index = [lax.rem(z + o, n_z) for o in range(1, n_z)]
    z_peers = [(dp, lat_of(zo, x, core)) for zo in z_index]
    fwd_peers = [
        partner,
        (dp, lat_of(z, x_pair, core)),
        (dp, lat_of(z, x_pair, 1 - core)),
    ]

    def enc_copy(i):
        cols = pl.ds(pl.multiple_of(i * WIDTH, WIDTH), WIDTH)
        return pltpu.make_async_copy(enc_ref.at[:, cols], wbuf.at[i], w_sem.at[i])

    def dec_slot(j):
        return lax.rem(j + slots - (slots - n_enc), slots) if slots > n_enc else lax.rem(j, slots)

    def dec_copy(j):
        cols = pl.ds(pl.multiple_of(j * WIDTH, WIDTH), WIDTH)
        s = dec_slot(j)
        return pltpu.make_async_copy(
            dec_ref.at[:, cols], wbuf.at[s, pl.ds(0, lat_dev)], w_sem.at[s]
        )

    def remote(src, dst, ssem, rsem, device):
        return pltpu.make_async_remote_copy(
            src_ref=src, dst_ref=dst, send_sem=ssem, recv_sem=rsem,
            device_id=device, device_id_type=MESH,
        )

    def start_enc(i, _):
        enc_copy(i).start()
        return 0

    lax.fori_loop(0, n_enc, start_enc, 0)
    ahead = slots - n_enc
    for j in range(ahead):
        dec_copy(j).start()
    own_rows = pl.ds(pl.multiple_of(dp * rows, rows), rows)
    local = pltpu.make_async_copy(resid_ref, xfull.at[own_rows], loc_sem)
    local.start()

    barrier = pltpu.get_barrier_semaphore()
    greeted = dp_peers + x_peers + z_peers + [fwd_peers[0], fwd_peers[2]]
    for device in greeted:
        pl.semaphore_signal(barrier, inc=1, device_id=device, device_id_type=MESH)
    pl.semaphore_wait(barrier, len(greeted))

    def gather(o, s):
        cols = pl.ds(s * piece, piece)
        src_rows = pl.ds(pl.multiple_of(core * h_rows, 16), h_rows)
        dst_rows = pl.ds(pl.multiple_of(dp * rows + core * h_rows, 16), h_rows)
        return remote(
            resid_ref.at[src_rows, cols], xfull.at[dst_rows, cols],
            g_ssem.at[o, s], g_rsem.at[o, s], dp_peers[o],
        )

    def forward(o, s):
        cols = pl.ds(s * piece, piece)
        origin = lax.rem(dp + n_dp - (o + 1), n_dp)
        r = pl.ds(pl.multiple_of(origin * rows + core * h_rows, 16), h_rows)
        return remote(
            xfull.at[r, cols], xfull.at[r, cols], f_ssem.at[o, s], f_rsem.at[o, s], partner
        )

    pairs = [(o, s) for s in range(PIECES) for o in range(n_dp - 1)]
    for o, s in pairs:
        gather(o, s).start()

    first_col = (dp * lax.axis_size("latent") + lat) * lat_dev
    columns = first_col + lax.broadcasted_iota(jnp.int32, (1, lat_dev), 1)
    thresh_all = thresh_ref[...]
    targets = jnp.full((1, lat_dev), no_target, jnp.float32)
    for k in range(ids_ref.shape[0]):
        level = levels_ref[k].astype(jnp.float32)
        targets = jnp.where(
            columns == ids_ref[k], jnp.maximum(targets, level * thresh_all), targets
        )
    targ[...] = targets

    for o, s in pairs:
        gather(o, s).wait_recv()
        forward(o, s).start()
    local.wait()
    for o, s in pairs:
        forward(o, s).wait_recv()

    def encode(i, _):
        cols = pl.ds(pl.multiple_of(i * WIDTH, WIDTH), WIDTH)
        enc_copy(i).wait()
        pre = jnp.dot(xfull[...], wbuf[i], preferred_element_type=jnp.float32) + bias_ref[:, cols]
        act = pre * jax.nn.sigmoid((pre - thresh_ref[:, cols]) / gate_width)
        acts[:, cols] = jnp.maximum(act, targ[:, cols]).astype(jnp.bfloat16)

        @pl.when(i + ahead < n_dec)
        def _():
            dec_copy(i + ahead).start()

        return 0

    lax.fori_loop(0, n_enc, encode, 0)

    def pair_copy(k):
        return remote(pair_tx.at[k], pair_rx.at[k], pair_ssem.at[k], pair_rsem.at[k], partner)

    def y_copy(k, o):
        return remote(
            y_tx.at[k, o], y_rx.at[k, o], y_ssem.at[k, o], y_rsem.at[k, o], dp_peers[o]
        )

    def x_copy(k, o):
        return remote(x_tx.at[k, o], x_rx.at[k, o], x_ssem.at[k, o], x_rsem.at[k, o], x_peers[o])

    def z_copy(k, o):
        return remote(z_tx.at[k, o], z_rx.at[k, o], z_ssem.at[k, o], z_rsem.at[k, o], z_peers[o])

    def own_cols(k):
        return pl.ds(pl.multiple_of(k * WIDTH + core * HALF + xh * QUART, QUART), QUART)

    def a_copy(k, o):
        ref = recon.at[pl.ds(pl.multiple_of(z * z_rows, 16), z_rows), own_cols(k)]
        return remote(ref, ref, a_ssem.at[k, o], a_rsem.at[k, o], z_peers[o])

    def b_copy(k, o):
        ref = recon.at[:, own_cols(k)]
        return remote(ref, ref, b_ssem.at[k, o], b_rsem.at[k, o], fwd_peers[o])

    def decode(k):
        dec_copy(k).wait()
        part = jnp.dot(
            acts[...], wbuf[dec_slot(k), :lat_dev], preferred_element_type=jnp.float32
        )
        low, high = part[:, :HALF], part[:, HALF:]
        own[lax.rem(k, LAGS[0] + 1)] = jnp.where(core == 0, low, high)
        pair_tx[k] = jnp.where(core == 0, high, low).astype(jnp.bfloat16)
        pair_copy(k).start()

        if n_enc + ahead < n_dec:

            @pl.when(k + n_enc + ahead < n_dec)
            def _():
                dec_copy(k + n_enc + ahead).start()

    def after_pair(k):
        pair_copy(k).wait_recv()
        slot = lax.rem(k, LAGS[0] + 1)

        def rows_of(q):
            r = pl.ds(pl.multiple_of(q * rows, rows), rows)
            return own[slot, r] + pair_rx[k, r].astype(jnp.float32)

        for o in range(n_dp - 1):
            y_tx[k, o] = rows_of(dp_peers[o][0]).astype(jnp.bfloat16)
            y_copy(k, o).start()
        y_own[k] = rows_of(dp)

    def after_y(k):
        total = y_own[k]
        for o in range(n_dp - 1):
            y_copy(k, o).wait_recv()
            total = total + y_rx[k, o].astype(jnp.float32)
        halves = (total[:, :QUART], total[:, QUART:])
        for o in range(n_x - 1):
            there = jnp.where(lax.rem(x_index[o], 2) == 0, halves[0], halves[1])
            x_tx[k, o] = there.astype(jnp.bfloat16)
            x_copy(k, o).start()
        x_own[k] = jnp.where(xh == 0, halves[0], halves[1])

    def after_x(k):
        total = x_own[k]
        for o in range(n_x - 1):
            x_copy(k, o).wait_recv()
            total = total + x_rx[k, o].astype(jnp.float32)
        x_own[k] = total
        for o in range(n_z - 1):
            r = pl.ds(pl.multiple_of(z_index[o] * z_rows, z_rows), z_rows)
            z_tx[k, o] = x_own[k, r].astype(jnp.bfloat16)
            z_copy(k, o).start()

    def after_z(k):
        total = x_own[k, pl.ds(pl.multiple_of(z * z_rows, z_rows), z_rows)]
        for o in range(n_z - 1):
            z_copy(k, o).wait_recv()
            total = total + z_rx[k, o].astype(jnp.float32)
        bias_row = k * (WIDTH // QUART) + core * (HALF // QUART) + xh
        total = total + dbias_ref[pl.ds(bias_row, 1), :]
        r = pl.ds(pl.multiple_of(z * z_rows, 16), z_rows)
        recon[r, own_cols(k)] = total.astype(jnp.bfloat16)
        for o in range(n_z - 1):
            a_copy(k, o).start()

    def after_gather(k):
        for o in range(n_z - 1):
            a_copy(k, o).wait_recv()
        for o in range(3):
            b_copy(k, o).start()

    stages = (after_pair, after_y, after_x, after_z, after_gather)

    def step(it, _):
        @pl.when(it < n_dec)
        def _():
            decode(it)

        for stage, lag in zip(stages, LAGS):

            @pl.when(jnp.logical_and(it >= lag, it < n_dec + lag))
            def _(stage=stage, lag=lag):
                stage(it - lag)

        return 0

    lax.fori_loop(0, n_dec + LAGS[-1], step, 0)

    resid32 = xfull[own_rows].astype(jnp.float32)
    in_sq = jnp.sum(jnp.square(resid32), axis=1, keepdims=True)

    def finish(k, _):
        for o in range(3):
            b_copy(k, o).wait_recv()
        return 0

    lax.fori_loop(0, n_dec, finish, 0)

    full = recon[...].astype(jnp.float32)
    out_sq = jnp.sum(jnp.square(full), axis=1, keepdims=True)
    scale = jnp.sqrt((in_sq + norm_eps) / (out_sq + norm_eps))
    out_ref[...] = (recon[...].astype(jnp.float32) * scale).astype(jnp.bfloat16)

    for o, s in pairs:
        gather(o, s).wait_send()
        forward(o, s).wait_send()

    def sent(k, _):
        pair_copy(k).wait_send()
        for o in range(n_dp - 1):
            y_copy(k, o).wait_send()
        for o in range(n_x - 1):
            x_copy(k, o).wait_send()
        for o in range(n_z - 1):
            z_copy(k, o).wait_send()
            a_copy(k, o).wait_send()
        for o in range(3):
            b_copy(k, o).wait_send()
        return 0

    lax.fori_loop(0, n_dec, sent, 0)


def body(n_dp, n_lat, resid, enc_weight, enc_bias, thresholds, dec_weight, dec_bias, ids, levels):
    rows, width = resid.shape
    lat_dev = enc_weight.shape[1]
    tokens = rows * n_dp
    n_enc, n_dec = lat_dev // WIDTH, width // WIDTH
    n_z = 4
    n_x = n_lat // (2 * n_z)
    slots = n_enc + 1 if tokens <= 256 else n_enc
    z_rows = rows // n_z
    bf16, f32 = jnp.bfloat16, jnp.float32
    dma = pltpu.SemaphoreType.DMA
    anywhere = pl.BlockSpec(memory_space=pl.ANY)
    vmem = pl.BlockSpec(memory_space=pltpu.VMEM)
    smem = pl.BlockSpec(memory_space=pltpu.SMEM)
    return pl.pallas_call(
        functools.partial(kernel, (n_dp, n_z, n_x, slots)),
        out_shape=jax.ShapeDtypeStruct((rows, width), bf16),
        in_specs=[smem, smem, anywhere, anywhere, vmem, vmem, anywhere, vmem],
        out_specs=vmem,
        scratch_shapes=[
            pltpu.VMEM((slots, width, WIDTH), bf16),
            pltpu.VMEM((tokens, width), bf16),
            pltpu.VMEM((tokens, lat_dev), bf16),
            pltpu.VMEM((1, lat_dev), f32),
            pltpu.VMEM((LAGS[0] + 1, tokens, HALF), f32),
            pltpu.VMEM((n_dec, tokens, HALF), bf16),
            pltpu.VMEM((n_dec, tokens, HALF), bf16),
            pltpu.VMEM((n_dec, rows, HALF), f32),
            pltpu.VMEM((n_dec, n_dp - 1, rows, HALF), bf16),
            pltpu.VMEM((n_dec, n_dp - 1, rows, HALF), bf16),
            pltpu.VMEM((n_dec, rows, QUART), f32),
            pltpu.VMEM((n_dec, n_x - 1, rows, QUART), bf16),
            pltpu.VMEM((n_dec, n_x - 1, rows, QUART), bf16),
            pltpu.VMEM((n_dec, n_z - 1, z_rows, QUART), bf16),
            pltpu.VMEM((n_dec, n_z - 1, z_rows, QUART), bf16),
            pltpu.VMEM((rows, width), bf16),
            dma((slots,)),
            dma,
            dma((n_dp - 1, PIECES)),
            dma((n_dp - 1, PIECES)),
            dma((n_dp - 1, PIECES)),
            dma((n_dp - 1, PIECES)),
            dma((n_dec,)),
            dma((n_dec,)),
            dma((n_dec, n_dp - 1)),
            dma((n_dec, n_dp - 1)),
            dma((n_dec, n_x - 1)),
            dma((n_dec, n_x - 1)),
            dma((n_dec, n_z - 1)),
            dma((n_dec, n_z - 1)),
            dma((n_dec, n_z - 1)),
            dma((n_dec, n_z - 1)),
            dma((n_dec, 3)),
            dma((n_dec, 3)),
        ],
        compiler_params=pltpu.CompilerParams(
            collective_id=0, has_side_effects=True, vmem_limit_bytes=60 * 2**20
        ),
    )(
        ids,
        levels,
        resid,
        enc_weight,
        enc_bias.reshape(1, lat_dev),
        thresholds.reshape(1, lat_dev),
        dec_weight,
        dec_bias.reshape(width // QUART, QUART),
    )


def solution(mesh):
    in_specs = (
        P("dp", None),
        P(None, ("dp", "latent")),
        P(("dp", "latent")),
        P(("dp", "latent")),
        P(("dp", "latent"), None),
        P(),
        P(),
        P(),
    )
    return jax.shard_map(
        functools.partial(body, mesh.shape["dp"], mesh.shape["latent"]),
        mesh=mesh,
        in_specs=in_specs,
        out_specs=P("dp", None),
        check_vma=False,
    )
```
